128 devices in a mesh: ctx: 64 (over z, y_hi, x, core), tp: 2 (over y_lo).
Axes of the slice: x: 4, y: 4 (y_hi: 2, y_lo: 2; y = y_hi * 2 + y_lo), z: 4, core: 2. Of those that a mesh axis runs over, the one named last changes fastest.
Arguments:
- query_gate: bfloat16 [32768, 4096], P('ctx', 'tp'), may hold values from -6 to 6
- key_gate: bfloat16 [32768, 4096], P('ctx', 'tp'), may hold values from -6 to 6
- value_input: bfloat16 [32768, 4096], P('ctx', 'tp'), may hold values from -6 to 6
- decay_rates: float32 [16, 4096], P(None, 'tp'), may hold values from 3.0517577e-07 to 0.05
- residues: float32 [16, 4096], P(None, 'tp'), may hold values from -1.5 to 1.5
- skip_gain: float32 [4096], P('tp'), may hold values from -4 to 4
- out_weight: bfloat16 [4096, 4096], P('tp'), may hold values from -0.09375 to 0.09375
Outputs:
- mixed: bfloat16 [32768, 4096], P('ctx', 'tp')
The draws below stay inside these ranges and needn't reach their ends.
All inputs are finite; a program needn't handle non-finite values.
Results may differ from the reference program's by a relative error of at most 0.005.
Values sent between devices are 32-bit elements; how exact they have to be, the bound alone decides.
A program may use at most 320 MiB of HBM per device.

```python
import math
import jax
import jax.numpy as jnp
from jax import lax

C = 4096
DOUT = 4096
ORDER = 16
BLK = 64
TOKENS = 32768


def steps_of(stream_key, shape, shards, least, top_value):
    def one(dim, blocks):
        draws = jax.random.uniform(jax.random.fold_in(jax.random.fold_in(stream_key, 6), dim), (blocks,), jnp.float32, least / len(shards), top_value / len(shards))
        return jnp.repeat(jnp.exp(draws), shape[dim] // blocks).reshape((-1,) + (1,) * (len(shape) - dim - 1))

    level = one(*shards[0])
    for cut in shards[1:]:
        level = level * one(*cut)
    return level


def noise(stream_key, dims, spread, bound, split=(), kind=jnp.bfloat16):
    gain = steps_of(stream_key, dims, split, -0.22, 0.18) if split else 1.0
    result = jax.random.normal(stream_key, dims, jnp.float32) * spread * gain
    return jnp.minimum(jnp.maximum(result, -bound), bound).astype(kind)


def setup_inputs(seed: int = 0) -> dict:
    seeds = jax.random.split(jax.random.key(seed), 8)
    query_gate = noise(seeds[0], (TOKENS, C), 1.0, 6.0, ((0, 64), (1, 2)))
    key_gate = noise(seeds[1], (TOKENS, C), 1.0, 6.0, ((0, 64), (1, 2)))
    value_input = noise(seeds[2], (TOKENS, C), 1.0, 6.0, ((0, 64), (1, 2)))
    decay_rates = jnp.clip(jnp.exp(math.log(0.05) - 12.006645658086184 * jax.random.uniform(seeds[3], (ORDER, C), jnp.float32) ** steps_of(seeds[3], (ORDER, C), ((1, 2),), -0.2, 0.2)), 3.0517577442878974e-07, 0.05)
    residues = noise(seeds[4], (ORDER, C), 0.25, 1.5, ((1, 2),), jnp.float32)
    skip_gain = noise(seeds[5], (C,), 1.0, 4.0, ((0, 2),), jnp.float32)
    out_weight = noise(seeds[6], (C, DOUT), C ** -0.5, 0.09375, ((0, 2),))
    return {"query_gate": query_gate, "key_gate": key_gate, "value_input": value_input, "decay_rates": decay_rates, "residues": residues, "skip_gain": skip_gain, "out_weight": out_weight}


def reference(query_gate, key_gate, value_input, decay_rates, residues, skip_gain, out_weight):
    highest = lax.Precision.HIGHEST
    product = key_gate.astype(jnp.float32) * value_input.astype(jnp.float32)
    blocks = TOKENS // BLK
    blocked = product.reshape(blocks, BLK, C)
    mode_gain = jnp.sqrt(-jnp.expm1(-2.0 * decay_rates))
    weighted = residues * mode_gain
    offsets = jnp.arange(BLK, dtype=jnp.float32)
    powers = jnp.exp(-offsets[:, None, None] * decay_rates[None])
    kernel = jnp.einsum('jnc,nc->jc', powers, weighted, precision=highest)
    distance = jnp.arange(BLK, dtype=jnp.int32)[:, None] - jnp.arange(BLK, dtype=jnp.int32)[None, :]
    toeplitz = jnp.where((distance >= 0)[:, :, None], kernel[jnp.maximum(distance, 0)], 0.0)
    inside = jnp.einsum('tsc,bsc->btc', toeplitz, blocked, precision=highest)
    feeder = jnp.exp(-(BLK - 1 - offsets)[:, None, None] * decay_rates[None])
    contrib = jnp.einsum('snc,bsc->bnc', feeder, blocked, precision=highest)
    step_decay = jnp.exp(-BLK * decay_rates)

    def advance(carried_state, block_term):
        return (step_decay * carried_state + block_term, carried_state)
    _, starts = lax.scan(advance, jnp.zeros((ORDER, C), jnp.float32), contrib)
    readout = jnp.exp(-(offsets + 1.0)[:, None, None] * decay_rates[None]) * weighted[None]
    carried = jnp.einsum('tnc,bnc->btc', readout, starts, precision=highest)
    filtered = (inside + carried).reshape(TOKENS, C)
    gated_out = (query_gate.astype(jnp.float32) * (filtered + skip_gain * product)).astype(jnp.bfloat16)
    return jnp.dot(gated_out, out_weight, preferred_element_type=jnp.float32).astype(jnp.bfloat16)
```

```python
import jax
import jax.numpy as jnp
from jax import lax
from jax.experimental import pallas as pl
from jax.experimental.pallas import tpu as pltpu
from jax.sharding import PartitionSpec as P

MESH = pl.DeviceIdType.MESH
F32 = jnp.float32
BF16 = jnp.bfloat16

ROWS = 512
CHAN = 2048
COLS = 2048
MODES = 16
LANES = 128
NB = 8
NJ = ROWS // NB
NCG = CHAN // LANES
SHARES = 8
CPS = NCG // SHARES
JPC = 8
NCHUNK = NJ // JPC
CROWS = JPC * NB
TILE = 512
NT = COLS // TILE
LPT = TILE // LANES


def one_minus_exp_neg(y):
    series = jnp.ones_like(y)
    for k in range(10, 1, -1):
        series = 1.0 - y * series * (1.0 / k)
    return jnp.where(y < 0.5, y * series, 1.0 - jnp.exp(-y))


def spread(x):
    return jnp.broadcast_to(x[:, None, :], (MODES, NB, LANES))


def kernel(
    q_hbm, k_hbm, v_hbm, lam_hbm, res_hbm, skip_hbm, w_hbm, out_hbm,
    qb, kb, vb, lam, res, skip, wv, prod, gate, gated, send_p, recv_p, own_p, out_v,
    a_s, w_s, pw_s, state, ends, recv1, recv2, recv3, send2, send3,
    in_sem, w_sem, out_sem, s1, r1, s2, r2, s3, r3, sp, rp,
):
    c = lax.axis_index("ctx")
    t = lax.axis_index("tp")
    member = lax.rem(c, 8)
    yh = lax.rem(c // 8, 2)
    z = c // 16
    group = z * 2 + yh
    base = c - member

    def member_dev(m):
        return (base + m, t)

    def group_dev(g):
        return (g * 8 + member, t)

    partner = (c, 1 - t)

    def lanes(cg):
        return pl.ds(pl.multiple_of(cg * LANES, LANES), LANES)

    def share_cols(s):
        return pl.ds(pl.multiple_of(s * (CPS * LANES), CPS * LANES), CPS * LANES)

    small = [
        pltpu.make_async_copy(lam_hbm, lam, in_sem.at[3, 0]),
        pltpu.make_async_copy(res_hbm, res, in_sem.at[3, 1]),
        pltpu.make_async_copy(skip_hbm, skip, in_sem.at[3, 2]),
    ]
    for cp in small:
        cp.start()

    def load(which, hbm, dst, s):
        return pltpu.make_async_copy(hbm.at[:, share_cols(s)], dst.at[:, share_cols(s)], in_sem.at[which, s])

    for s in range(SHARES):
        load(0, k_hbm, kb, s).start()
        load(1, v_hbm, vb, s).start()

    barrier = pltpu.get_barrier_semaphore()
    for i in range(1, 8):
        pl.semaphore_signal(barrier, inc=1, device_id=member_dev(lax.rem(member + i, 8)), device_id_type=MESH)
        pl.semaphore_signal(barrier, inc=1, device_id=group_dev(lax.rem(group + i, 8)), device_id_type=MESH)
    pl.semaphore_signal(barrier, inc=1, device_id=partner, device_id_type=MESH)

    for cp in small:
        cp.wait()
    pl.semaphore_wait(barrier, 15)

    sub = lax.broadcasted_iota(jnp.int32, (MODES, NB, LANES), 1)

    def first_pass(s, _):
        load(0, k_hbm, kb, s).wait()
        load(1, v_hbm, vb, s).wait()

        def group_pass(u, _):
            cg = s * CPS + u
            cols = lanes(cg)
            rate = lam[:, cols]
            a = spread(jnp.exp(-rate))
            a_s[cg] = a
            for b in range(NB):
                rows = pl.ds(b * NJ, NJ)
                prod[cg, pl.ds(b, NJ, stride=NB), :] = kb[rows, cols].astype(F32) * vb[rows, cols].astype(F32)

            def step(j, acc):
                p = prod[cg, pl.ds(pl.multiple_of(j * NB, NB), NB), :]
                return acc * a + p[None]

            acc = lax.fori_loop(0, NJ, step, jnp.zeros((MODES, NB, LANES), F32), unroll=8)
            d1 = spread(jnp.exp(-float(NJ) * rate))
            d2 = d1 * d1
            acc = acc + jnp.where(sub >= 1, d1 * pltpu.roll(acc, 1, 1), 0.0)
            acc = acc + jnp.where(sub >= 2, d2 * pltpu.roll(acc, 2, 1), 0.0)
            acc = acc + jnp.where(sub >= 4, d2 * d2 * pltpu.roll(acc, 4, 1), 0.0)
            state[cg] = jnp.where(sub >= 1, pltpu.roll(acc, 1, 1), 0.0)
            ends[s, u] = acc[:, NB - 1, :]
            return 0

        lax.fori_loop(0, CPS, group_pass, 0)

        @pl.when(s != member)
        def _():
            pltpu.make_async_remote_copy(
                src_ref=ends.at[s], dst_ref=recv1.at[member], send_sem=s1.at[s], recv_sem=r1.at[member],
                device_id=member_dev(s), device_id_type=MESH,
            ).start()

        @pl.when(s == member)
        def _():
            recv1[member] = ends[s]

        return 0

    lax.fori_loop(0, SHARES, first_pass, 0)

    def load_w(half, n):
        start = (1 - t if half == 0 else t) * COLS + n * TILE
        cols = pl.ds(pl.multiple_of(start, TILE), TILE)
        return pltpu.make_async_copy(w_hbm.at[:, cols], wv.at[half, n], w_sem.at[half, n])

    for s in range(SHARES):
        load(2, q_hbm, qb, s).start()
    for half in range(2):
        for n in range(NT):
            load_w(half, n).start()

    def share_decay(span):
        return jnp.exp(-float(span) * lam[:, share_cols(member)])

    def halves(x):
        return jnp.stack([x[:, u * LANES:(u + 1) * LANES] for u in range(CPS)])

    d_dev = halves(share_decay(ROWS))
    d_grp = halves(share_decay(ROWS * 8))

    def wait_recv(buf, sem, i, ssem):
        pltpu.make_async_remote_copy(
            src_ref=buf.at[i], dst_ref=buf.at[i], send_sem=ssem.at[i], recv_sem=sem.at[i],
            device_id=partner, device_id_type=MESH,
        ).wait_recv()

    for i in range(1, 8):
        m = lax.rem(member + i, 8)
        wait_recv(recv1, r1, m, s1)
    total = recv1[0]
    for m in range(1, 8):
        total = total * d_dev + recv1[m]
    send2[...] = total
    recv2[group] = total

    def copy2(g):
        return pltpu.make_async_remote_copy(
            src_ref=send2, dst_ref=recv2.at[group], send_sem=s2.at[g], recv_sem=r2.at[group],
            device_id=group_dev(g), device_id_type=MESH,
        )

    for i in (4, 5, 3, 6, 2, 7, 1):
        copy2(lax.rem(group + i, 8)).start()

    def prepare(cg, _):
        cols = lanes(cg)
        rate = lam[:, cols]
        w_s[cg] = spread(res[:, cols] * jnp.sqrt(one_minus_exp_neg(2.0 * rate)))
        pw_s[cg] = jnp.exp(spread(rate) * (sub.astype(F32) * -float(NJ)))
        for b in range(NB):
            gate[cg, pl.ds(b, NJ, stride=NB), :] = qb[pl.ds(b * NJ, NJ), cols].astype(F32)
        return 0

    for s in range(SHARES):
        load(2, q_hbm, qb, s).wait()
    lax.fori_loop(0, NCG, prepare, 0)

    for i in (1, 7, 2, 6, 3, 5, 4):
        wait_recv(recv2, r2, lax.rem(group + i, 8), s2)
    incoming = jnp.zeros((CPS, MODES, LANES), F32)
    for g in range(8):
        incoming = jnp.where(g < group, incoming * d_grp + recv2[g], incoming)
    for m in range(8):
        send3[m] = incoming
        if m < 7:
            incoming = incoming * d_dev + recv1[m]
    recv3[member] = send3[member]

    def copy3(m):
        return pltpu.make_async_remote_copy(
            src_ref=send3.at[m], dst_ref=recv3.at[member], send_sem=s3.at[m], recv_sem=r3.at[member],
            device_id=member_dev(m), device_id_type=MESH,
        )

    for i in (4, 5, 3, 6, 2, 7, 1):
        copy3(lax.rem(member + i, 8)).start()

    def second_pass(chunk, cg):
        cols = lanes(cg)
        a = a_s[cg]
        w = w_s[cg]
        gain = skip[:, cols]
        x = state[cg]
        for pair in range(JPC // 2):
            tiles = []
            for j in (2 * pair, 2 * pair + 1):
                rows = pl.ds(pl.multiple_of((chunk * JPC + j) * NB, NB), NB)
                p = prod[cg, rows, :]
                x = x * a + p[None]
                filtered = jnp.sum(x * w, axis=0) + gain * p
                tiles.append(gate[cg, rows, :] * filtered)
            rows = pl.ds(pl.multiple_of(chunk * CROWS + pair * 16, 16), 16)
            gated[rows, cols] = jnp.concatenate(tiles, axis=0).astype(BF16)
        state[cg] = x

    def chunk_rows(chunk):
        return pl.ds(pl.multiple_of(chunk * CROWS, CROWS), CROWS)

    def tile_lanes(n):
        return pl.ds(n * LPT, LPT)

    def piece(chunk, n):
        return pltpu.make_async_remote_copy(
            src_ref=send_p.at[tile_lanes(n), chunk_rows(chunk)], dst_ref=recv_p.at[tile_lanes(n), chunk_rows(chunk)],
            send_sem=sp.at[chunk, n], recv_sem=rp.at[chunk, n], device_id=partner, device_id_type=MESH,
        )

    def project(chunk):
        rows = chunk_rows(chunk)

        def other(n, _):
            sums = jnp.dot(gated[rows, :], wv[0, n], preferred_element_type=F32)
            for u in range(LPT):
                send_p[n * LPT + u, rows, :] = sums[:, u * LANES:(u + 1) * LANES]
            piece(chunk, n).start()
            return 0

        lax.fori_loop(0, NT, other, 0)

    def project_own(chunk):
        rows = chunk_rows(chunk)

        def own(n, _):
            sums = jnp.dot(gated[rows, :], wv[1, n], preferred_element_type=F32)
            for u in range(LPT):
                own_p[n * LPT + u, rows, :] = sums[:, u * LANES:(u + 1) * LANES]
            return 0

        lax.fori_loop(0, NT, own, 0)

    for i in range(8):
        s = lax.rem(member + i, 8)
        if i > 0:
            wait_recv(recv3, r3, s, s3)

        def start(u, _, s=s):
            cg = s * CPS + u
            state[cg] = state[cg] + pw_s[cg] * spread(recv3[s, u])
            second_pass(0, cg)
            return 0

        lax.fori_loop(0, CPS, start, 0)

    for n in range(NT):
        load_w(0, n).wait()
    project(0)
    for n in range(NT):
        load_w(1, n).wait()
    project_own(0)

    def chunk_step(chunk, _):
        def one(cg, _):
            second_pass(chunk, cg)
            return 0

        lax.fori_loop(0, NCG, one, 0)
        project(chunk)
        project_own(chunk)
        return 0

    lax.fori_loop(1, NCHUNK, chunk_step, 0)

    def store(h, n):
        cols = pl.ds(pl.multiple_of(n * TILE, TILE), TILE)
        rows = pl.ds(pl.multiple_of(h * 16, 16), 16)
        return pltpu.make_async_copy(out_v.at[:, rows, cols], out_hbm.at[:, rows, cols], out_sem.at[h, n])

    def finish(i, _):
        h, n = i // NT, lax.rem(i, NT)
        cols = pl.ds(pl.multiple_of(n * TILE, TILE), TILE)
        piece(2 * h, n).wait_recv()
        piece(2 * h + 1, n).wait_recv()

        for u in range(LPT):
            k = n * LPT + u
            for b in range(NB):
                rows = pl.ds(h * (2 * CROWS) + b, 16, stride=NB)
                out_v[b, pl.ds(pl.multiple_of(h * 16, 16), 16), lanes(k)] = (own_p[k, rows, :] + recv_p[k, rows, :]).astype(BF16)
        store(h, n).start()
        return 0

    lax.fori_loop(0, (NCHUNK // 2) * NT, finish, 0)

    for i in range(1, 8):
        m = lax.rem(member + i, 8)
        g = lax.rem(group + i, 8)
        pltpu.make_async_remote_copy(
            src_ref=ends.at[m], dst_ref=recv1.at[member], send_sem=s1.at[m], recv_sem=r1.at[member],
            device_id=member_dev(m), device_id_type=MESH,
        ).wait_send()
        copy2(g).wait_send()
        copy3(m).wait_send()

    def drain(i, _):
        piece(i // NT, lax.rem(i, NT)).wait_send()
        return 0

    lax.fori_loop(0, NCHUNK * NT, drain, 0)

    def stored(i, _):
        store(i // NT, lax.rem(i, NT)).wait()
        return 0

    lax.fori_loop(0, (NCHUNK // 2) * NT, stored, 0)


def per_device(query_gate, key_gate, value_input, decay_rates, residues, skip_gain, out_weight):
    dma = pltpu.SemaphoreType.DMA
    out = pl.pallas_call(
        kernel,
        out_shape=jax.ShapeDtypeStruct((NB, NJ, COLS), BF16),
        in_specs=[pl.BlockSpec(memory_space=pl.ANY)] * 7,
        out_specs=pl.BlockSpec(memory_space=pl.ANY),
        scratch_shapes=[
            pltpu.VMEM((ROWS, CHAN), BF16),
            pltpu.VMEM((ROWS, CHAN), BF16),
            pltpu.VMEM((ROWS, CHAN), BF16),
            pltpu.VMEM((MODES, CHAN), F32),
            pltpu.VMEM((MODES, CHAN), F32),
            pltpu.VMEM((1, CHAN), F32),
            pltpu.VMEM((2, NT, CHAN, TILE), BF16),
            pltpu.VMEM((NCG, ROWS, LANES), F32),
            pltpu.VMEM((NCG, ROWS, LANES), F32),
            pltpu.VMEM((ROWS, CHAN), BF16),
            pltpu.VMEM((COLS // LANES, ROWS, LANES), F32),
            pltpu.VMEM((COLS // LANES, ROWS, LANES), F32),
            pltpu.VMEM((COLS // LANES, ROWS, LANES), F32),
            pltpu.VMEM((NB, NJ, COLS), BF16),
            pltpu.VMEM((NCG, MODES, NB, LANES), F32),
            pltpu.VMEM((NCG, MODES, NB, LANES), F32),
            pltpu.VMEM((NCG, MODES, NB, LANES), F32),
            pltpu.VMEM((NCG, MODES, NB, LANES), F32),
            pltpu.VMEM((SHARES, CPS, MODES, LANES), F32),
            pltpu.VMEM((8, CPS, MODES, LANES), F32),
            pltpu.VMEM((8, CPS, MODES, LANES), F32),
            pltpu.VMEM((8, CPS, MODES, LANES), F32),
            pltpu.VMEM((CPS, MODES, LANES), F32),
            pltpu.VMEM((8, CPS, MODES, LANES), F32),
            dma((4, SHARES)), dma((2, NT)), dma((NCHUNK // 2, NT)),
            dma((8,)), dma((8,)), dma((8,)), dma((8,)), dma((8,)), dma((8,)),
            dma((NCHUNK, NT)), dma((NCHUNK, NT)),
        ],
        compiler_params=pltpu.CompilerParams(
            collective_id=0, has_side_effects=True, vmem_limit_bytes=60 * 2**20
        ),
    )(
        query_gate, key_gate, value_input, decay_rates, residues, skip_gain.reshape(1, CHAN), out_weight
    )
    return out.reshape(ROWS, COLS)


def solution(mesh):
    in_specs = (
        P("ctx", "tp"),
        P("ctx", "tp"),
        P("ctx", "tp"),
        P(None, "tp"),
        P(None, "tp"),
        P("tp"),
        P("tp", None),
    )
    return jax.shard_map(per_device, mesh=mesh, in_specs=in_specs, out_specs=P("ctx", "tp"), check_vma=False)
```

```python
import jax
import jax.numpy as jnp
from jax import lax
from jax.experimental import pallas as pl
from jax.experimental.pallas import tpu as pltpu
from jax.sharding import PartitionSpec as P

MESH = pl.DeviceIdType.MESH
F32 = jnp.float32
BF16 = jnp.bfloat16

ROWS = 512
CHAN = 2048
COLS = 2048
MODES = 16
LANES = 128
NB = 8
NJ = ROWS // NB
NCG = CHAN // LANES
SHARES = 8
CPS = NCG // SHARES
JPC = 8
NCHUNK = NJ // JPC
CROWS = JPC * NB
TILE = 512
NT = COLS // TILE
LPT = TILE // LANES
EARLY = 4
SPLIT1, SPLIT2 = 6, 15


def one_minus_exp_neg(y):
    series = jnp.ones_like(y)
    for k in range(10, 1, -1):
        series = 1.0 - y * series * (1.0 / k)
    return jnp.where(y < 0.5, y * series, 1.0 - jnp.exp(-y))


def spread(x):
    return jnp.broadcast_to(x[:, None, :], (MODES, NB, LANES))


def kernel(
    q_hbm, k_hbm, v_hbm, lam_hbm, res_hbm, skip_hbm, w_hbm, out_v,
    qb, kb, vb, lam, res, skip, wv, prod, gate, gated, send_p, recv_p, own_p,
    a_s, w_s, pw_s, state, ends, recv1, recv2, recv3, send2, send3,
    in_sem, w_sem, s1, r1, s2, r2, s3, r3, sp, rp,
):
    c = lax.axis_index("ctx")
    t = lax.axis_index("tp")
    member = lax.rem(c, 8)
    yh = lax.rem(c // 8, 2)
    z = c // 16
    group = z * 2 + yh
    base = c - member

    def member_dev(m):
        return (base + m, t)

    def group_dev(g):
        return (g * 8 + member, t)

    partner = (c, 1 - t)

    def lanes(cg):
        return pl.ds(pl.multiple_of(cg * LANES, LANES), LANES)

    def share_cols(s):
        return pl.ds(pl.multiple_of(s * (CPS * LANES), CPS * LANES), CPS * LANES)

    small = [
        pltpu.make_async_copy(lam_hbm, lam, in_sem.at[3, 0]),
        pltpu.make_async_copy(res_hbm, res, in_sem.at[3, 1]),
        pltpu.make_async_copy(skip_hbm, skip, in_sem.at[3, 2]),
    ]
    for cp in small:
        cp.start()

    def load(which, hbm, dst, s):
        return pltpu.make_async_copy(hbm.at[:, share_cols(s)], dst.at[:, share_cols(s)], in_sem.at[which, s])

    for s in range(SHARES):
        load(0, k_hbm, kb, s).start()
        load(1, v_hbm, vb, s).start()

    barrier = pltpu.get_barrier_semaphore()
    for i in range(1, 8):
        pl.semaphore_signal(barrier, inc=1, device_id=member_dev(lax.rem(member + i, 8)), device_id_type=MESH)
        pl.semaphore_signal(barrier, inc=1, device_id=group_dev(lax.rem(group + i, 8)), device_id_type=MESH)
    pl.semaphore_signal(barrier, inc=1, device_id=partner, device_id_type=MESH)

    for cp in small:
        cp.wait()

    sub = lax.broadcasted_iota(jnp.int32, (MODES, NB, LANES), 1)

    def end_state(s):
        load(0, k_hbm, kb, s).wait()
        load(1, v_hbm, vb, s).wait()

        def group_pass(u, _):
            cols = lanes(s * CPS + u)
            rate = lam[:, cols]
            a8 = spread(jnp.exp(-8.0 * rate))

            def step(i, acc):
                rows = pl.ds(pl.multiple_of(i * 16, 16), 16)
                p = kb[rows, cols].astype(F32) * vb[rows, cols].astype(F32)
                acc = acc * a8 + p[None, :8]
                return acc * a8 + p[None, 8:]

            acc = lax.fori_loop(0, ROWS // 16, step, jnp.zeros((MODES, NB, LANES), F32), unroll=8)
            ends[s, u] = jnp.sum(acc * jnp.exp(spread(rate) * (sub - 7).astype(F32)), axis=1)
            return 0

        lax.fori_loop(0, CPS, group_pass, 0)

    def give_share(s):
        @pl.when(s != member)
        def _():
            pltpu.make_async_remote_copy(
                src_ref=ends.at[s], dst_ref=recv1.at[member], send_sem=s1.at[s], recv_sem=r1.at[member],
                device_id=member_dev(s), device_id_type=MESH,
            ).start()

        @pl.when(s == member)
        def _():
            recv1[member] = ends[s]

    def first_half(s, _):
        end_state(s)
        return 0

    def second_half(s, _):
        end_state(s)
        give_share(s)
        return 0

    lax.fori_loop(0, EARLY, first_half, 0)
    pl.semaphore_wait(barrier, 15)
    for s in range(EARLY):
        give_share(s)

    def load_w(half, n):
        start = (1 - t if half == 0 else t) * COLS + n * TILE
        cols = pl.ds(pl.multiple_of(start, TILE), TILE)
        return pltpu.make_async_copy(w_hbm.at[:, cols], wv.at[half, n], w_sem.at[half, n])

    for s in range(SHARES):
        load(2, q_hbm, qb, s).start()
    for half in range(2):
        for n in range(NT):
            load_w(half, n).start()

    lax.fori_loop(EARLY, SHARES, second_half, 0)

    def block_states(cg, _):
        cols = lanes(cg)
        rate = lam[:, cols]
        a = spread(jnp.exp(-rate))
        a_s[cg] = a
        for b in range(NB):
            rows = pl.ds(b * NJ, NJ)
            prod[cg, pl.ds(b, NJ, stride=NB), :] = kb[rows, cols].astype(F32) * vb[rows, cols].astype(F32)

        def step(j, acc):
            p = prod[cg, pl.ds(pl.multiple_of(j * NB, NB), NB), :]
            return acc * a + p[None]

        acc = lax.fori_loop(0, NJ, step, jnp.zeros((MODES, NB, LANES), F32), unroll=16)
        d1 = spread(jnp.exp(-float(NJ) * rate))
        d2 = d1 * d1
        acc = acc + jnp.where(sub >= 1, d1 * pltpu.roll(acc, 1, 1), 0.0)
        acc = acc + jnp.where(sub >= 2, d2 * pltpu.roll(acc, 2, 1), 0.0)
        acc = acc + jnp.where(sub >= 4, d2 * d2 * pltpu.roll(acc, 4, 1), 0.0)
        state[cg] = jnp.where(sub >= 1, pltpu.roll(acc, 1, 1), 0.0)
        return 0

    lax.fori_loop(0, SPLIT1, block_states, 0)

    def share_decay(span):
        return jnp.exp(-float(span) * lam[:, share_cols(member)])

    def halves(x):
        return jnp.stack([x[:, u * LANES:(u + 1) * LANES] for u in range(CPS)])

    d_dev = halves(share_decay(ROWS))
    d_grp = halves(share_decay(ROWS * 8))

    def wait_recv(buf, sem, i, ssem):
        pltpu.make_async_remote_copy(
            src_ref=buf.at[i], dst_ref=buf.at[i], send_sem=ssem.at[i], recv_sem=sem.at[i],
            device_id=partner, device_id_type=MESH,
        ).wait_recv()

    for i in range(1, 8):
        m = lax.rem(member + i, 8)
        wait_recv(recv1, r1, m, s1)
    total = recv1[0]
    for m in range(1, 8):
        total = total * d_dev + recv1[m]
    send2[...] = total
    recv2[group] = total

    def copy2(g):
        return pltpu.make_async_remote_copy(
            src_ref=send2, dst_ref=recv2.at[group], send_sem=s2.at[g], recv_sem=r2.at[group],
            device_id=group_dev(g), device_id_type=MESH,
        )

    for i in (4, 5, 3, 6, 2, 7, 1):
        copy2(lax.rem(group + i, 8)).start()

    lax.fori_loop(SPLIT1, SPLIT2, block_states, 0)

    for i in (1, 7, 2, 6, 3, 5, 4):
        wait_recv(recv2, r2, lax.rem(group + i, 8), s2)
    incoming = jnp.zeros((CPS, MODES, LANES), F32)
    for g in range(8):
        incoming = jnp.where(g < group, incoming * d_grp + recv2[g], incoming)
    for m in range(8):
        send3[m] = incoming
        if m < 7:
            incoming = incoming * d_dev + recv1[m]
    recv3[member] = send3[member]

    def copy3(m):
        return pltpu.make_async_remote_copy(
            src_ref=send3.at[m], dst_ref=recv3.at[member], send_sem=s3.at[m], recv_sem=r3.at[member],
            device_id=member_dev(m), device_id_type=MESH,
        )

    for i in (4, 5, 3, 6, 2, 7, 1):
        copy3(lax.rem(member + i, 8)).start()

    lax.fori_loop(SPLIT2, NCG, block_states, 0)

    def prepare(cg, _):
        cols = lanes(cg)
        rate = lam[:, cols]
        w_s[cg] = spread(res[:, cols] * jnp.sqrt(one_minus_exp_neg(2.0 * rate)))
        pw_s[cg] = jnp.exp(spread(rate) * (sub.astype(F32) * -float(NJ)))
        for b in range(NB):
            gate[cg, pl.ds(b, NJ, stride=NB), :] = qb[pl.ds(b * NJ, NJ), cols].astype(F32)
        return 0

    for s in range(SHARES):
        load(2, q_hbm, qb, s).wait()
    lax.fori_loop(0, NCG, prepare, 0)

    def second_pass(chunk, cg):
        cols = lanes(cg)
        a = a_s[cg]
        w = w_s[cg]
        gain = skip[:, cols]
        x = state[cg]
        for pair in range(JPC // 2):
            tiles = []
            for j in (2 * pair, 2 * pair + 1):
                rows = pl.ds(pl.multiple_of((chunk * JPC + j) * NB, NB), NB)
                p = prod[cg, rows, :]
                x = x * a + p[None]
                filtered = jnp.sum(x * w, axis=0) + gain * p
                tiles.append(gate[cg, rows, :] * filtered)
            rows = pl.ds(pl.multiple_of(chunk * CROWS + pair * 16, 16), 16)
            gated[rows, cols] = jnp.concatenate(tiles, axis=0).astype(BF16)
        state[cg] = x

    def chunk_rows(chunk):
        return pl.ds(pl.multiple_of(chunk * CROWS, CROWS), CROWS)

    def tile_lanes(n):
        return pl.ds(n * LPT, LPT)

    def piece(chunk, n):
        return pltpu.make_async_remote_copy(
            src_ref=send_p.at[tile_lanes(n), chunk_rows(chunk)], dst_ref=recv_p.at[tile_lanes(n), chunk_rows(chunk)],
            send_sem=sp.at[chunk, n], recv_sem=rp.at[chunk, n], device_id=partner, device_id_type=MESH,
        )

    def project(chunk):
        rows = chunk_rows(chunk)

        def other(n, _):
            sums = jnp.dot(gated[rows, :], wv[0, n], preferred_element_type=F32)
            for u in range(LPT):
                send_p[n * LPT + u, rows, :] = sums[:, u * LANES:(u + 1) * LANES]
            piece(chunk, n).start()
            return 0

        lax.fori_loop(0, NT, other, 0)

    def project_own(chunk):
        rows = chunk_rows(chunk)

        def own(n, _):
            sums = jnp.dot(gated[rows, :], wv[1, n], preferred_element_type=F32)
            for u in range(LPT):
                own_p[n * LPT + u, rows, :] = sums[:, u * LANES:(u + 1) * LANES]
            return 0

        lax.fori_loop(0, NT, own, 0)

    for i in range(8):
        s = lax.rem(member + i, 8)
        if i > 0:
            wait_recv(recv3, r3, s, s3)

        def start(u, _, s=s):
            cg = s * CPS + u
            state[cg] = state[cg] + pw_s[cg] * spread(recv3[s, u])
            second_pass(0, cg)
            return 0

        lax.fori_loop(0, CPS, start, 0)

    for n in range(NT):
        load_w(0, n).wait()
    project(0)
    for n in range(NT):
        load_w(1, n).wait()
    project_own(0)

    def chunk_step(chunk, _):
        def one(cg, _):
            second_pass(chunk, cg)
            return 0

        lax.fori_loop(0, NCG, one, 0)
        project(chunk)
        project_own(chunk)
        return 0

    lax.fori_loop(1, NCHUNK, chunk_step, 0)

    def finish(i, _):
        h, n = i // NT, lax.rem(i, NT)
        piece(2 * h, n).wait_recv()
        piece(2 * h + 1, n).wait_recv()

        for u in range(LPT):
            k = n * LPT + u
            for b in range(NB):
                rows = pl.ds(h * (2 * CROWS) + b, 16, stride=NB)
                out_v[b, pl.ds(pl.multiple_of(h * 16, 16), 16), lanes(k)] = (own_p[k, rows, :] + recv_p[k, rows, :]).astype(BF16)
        return 0

    lax.fori_loop(0, (NCHUNK // 2) * NT, finish, 0)

    for i in range(1, 8):
        m = lax.rem(member + i, 8)
        g = lax.rem(group + i, 8)
        pltpu.make_async_remote_copy(
            src_ref=ends.at[m], dst_ref=recv1.at[member], send_sem=s1.at[m], recv_sem=r1.at[member],
            device_id=member_dev(m), device_id_type=MESH,
        ).wait_send()
        copy2(g).wait_send()
        copy3(m).wait_send()

    def drain(i, _):
        piece(i // NT, lax.rem(i, NT)).wait_send()
        return 0

    lax.fori_loop(0, NCHUNK * NT, drain, 0)


def per_device(query_gate, key_gate, value_input, decay_rates, residues, skip_gain, out_weight):
    dma = pltpu.SemaphoreType.DMA
    out = pl.pallas_call(
        kernel,
        out_shape=pltpu.VMEM((NB, NJ, COLS), BF16),
        in_specs=[pl.BlockSpec(memory_space=pl.ANY)] * 7,
        out_specs=pl.BlockSpec(memory_space=pltpu.VMEM),
        scratch_shapes=[
            pltpu.VMEM((ROWS, CHAN), BF16),
            pltpu.VMEM((ROWS, CHAN), BF16),
            pltpu.VMEM((ROWS, CHAN), BF16),
            pltpu.VMEM((MODES, CHAN), F32),
            pltpu.VMEM((MODES, CHAN), F32),
            pltpu.VMEM((1, CHAN), F32),
            pltpu.VMEM((2, NT, CHAN, TILE), BF16),
            pltpu.VMEM((NCG, ROWS, LANES), F32),
            pltpu.VMEM((NCG, ROWS, LANES), F32),
            pltpu.VMEM((ROWS, CHAN), BF16),
            pltpu.VMEM((COLS // LANES, ROWS, LANES), F32),
            pltpu.VMEM((COLS // LANES, ROWS, LANES), F32),
            pltpu.VMEM((COLS // LANES, ROWS, LANES), F32),
            pltpu.VMEM((NCG, MODES, NB, LANES), F32),
            pltpu.VMEM((NCG, MODES, NB, LANES), F32),
            pltpu.VMEM((NCG, MODES, NB, LANES), F32),
            pltpu.VMEM((NCG, MODES, NB, LANES), F32),
            pltpu.VMEM((SHARES, CPS, MODES, LANES), F32),
            pltpu.VMEM((8, CPS, MODES, LANES), F32),
            pltpu.VMEM((8, CPS, MODES, LANES), F32),
            pltpu.VMEM((8, CPS, MODES, LANES), F32),
            pltpu.VMEM((CPS, MODES, LANES), F32),
            pltpu.VMEM((8, CPS, MODES, LANES), F32),
            dma((4, SHARES)), dma((2, NT)),
            dma((8,)), dma((8,)), dma((8,)), dma((8,)), dma((8,)), dma((8,)),
            dma((NCHUNK, NT)), dma((NCHUNK, NT)),
        ],
        compiler_params=pltpu.CompilerParams(
            collective_id=0, has_side_effects=True, vmem_limit_bytes=56 * 2**20
        ),
    )(
        query_gate, key_gate, value_input, decay_rates, residues, skip_gain.reshape(1, CHAN), out_weight
    )
    return out.reshape(ROWS, COLS)


def solution(mesh):
    in_specs = (
        P("ctx", "tp"),
        P("ctx", "tp"),
        P("ctx", "tp"),
        P(None, "tp"),
        P(None, "tp"),
        P("tp"),
        P("tp", None),
    )
    return jax.shard_map(per_device, mesh=mesh, in_specs=in_specs, out_specs=P("ctx", "tp"), check_vma=False)
```

```python
import jax
import jax.numpy as jnp
from jax import lax
from jax.experimental import pallas as pl
from jax.experimental.pallas import tpu as pltpu
from jax.sharding import PartitionSpec as P

MESH = pl.DeviceIdType.MESH
F32 = jnp.float32
BF16 = jnp.bfloat16

ROWS = 512
CHAN = 2048
COLS = 2048
MODES = 16
LANES = 128
NB = 8
NJ = ROWS // NB
NCG = CHAN // LANES
SHARES = 8
CPS = NCG // SHARES
JPC = 8
NCHUNK = NJ // JPC
CROWS = JPC * NB
TILE = 512
NT = COLS // TILE
LPT = TILE // LANES
EARLY = 4
SPLIT1, SPLIT2 = 6, 15


def one_minus_exp_neg(y):
    series = jnp.ones_like(y)
    for k in range(10, 1, -1):
        series = 1.0 - y * series * (1.0 / k)
    return jnp.where(y < 0.5, y * series, 1.0 - jnp.exp(-y))


def spread(x):
    return jnp.broadcast_to(x[:, None, :], (MODES, NB, LANES))


def kernel(
    q_hbm, k_hbm, v_hbm, lam_hbm, res_hbm, skip_hbm, w_hbm, out_v,
    qb, kb, vb, lam, res, skip, wv, prod, gate, gated, send_p, recv_p, own_p,
    a_s, w_s, pw_s, state, ends, recv1, recv2, recv3, send2, send3,
    in_sem, w_sem, s1, r1, s2, r2, s3, r3, sp, rp,
):
    c = lax.axis_index("ctx")
    t = lax.axis_index("tp")
    member = lax.rem(c, 8)
    yh = lax.rem(c // 8, 2)
    z = c // 16
    group = z * 2 + yh
    base = c - member

    def member_dev(m):
        return (base + m, t)

    def group_dev(g):
        return (g * 8 + member, t)

    partner = (c, 1 - t)

    def lanes(cg):
        return pl.ds(pl.multiple_of(cg * LANES, LANES), LANES)

    def share_cols(s):
        return pl.ds(pl.multiple_of(s * (CPS * LANES), CPS * LANES), CPS * LANES)

    small = [
        pltpu.make_async_copy(lam_hbm, lam, in_sem.at[3, 0]),
        pltpu.make_async_copy(res_hbm, res, in_sem.at[3, 1]),
        pltpu.make_async_copy(skip_hbm, skip, in_sem.at[3, 2]),
    ]
    for cp in small:
        cp.start()

    def load(which, hbm, dst, s):
        return pltpu.make_async_copy(hbm.at[:, share_cols(s)], dst.at[:, share_cols(s)], in_sem.at[which, s])

    for s in range(SHARES):
        load(0, k_hbm, kb, s).start()
        load(1, v_hbm, vb, s).start()

    barrier = pltpu.get_barrier_semaphore()
    for i in range(1, 8):
        pl.semaphore_signal(barrier, inc=1, device_id=member_dev(lax.rem(member + i, 8)), device_id_type=MESH)
        pl.semaphore_signal(barrier, inc=1, device_id=group_dev(lax.rem(group + i, 8)), device_id_type=MESH)
    pl.semaphore_signal(barrier, inc=1, device_id=partner, device_id_type=MESH)

    for cp in small:
        cp.wait()

    sub = lax.broadcasted_iota(jnp.int32, (MODES, NB, LANES), 1)

    def end_state(s):
        load(0, k_hbm, kb, s).wait()
        load(1, v_hbm, vb, s).wait()

        def group_pass(u, _):
            cols = lanes(s * CPS + u)
            rate = lam[:, cols]
            a8 = spread(jnp.exp(-8.0 * rate))
            a16 = a8 * a8

            def step(i, acc):
                rows = pl.ds(pl.multiple_of(i * 16, 16), 16)
                p = kb[rows, cols].astype(F32) * vb[rows, cols].astype(F32)
                return acc * a16 + (p[None, :8] * a8 + p[None, 8:])

            acc = lax.fori_loop(0, ROWS // 16, step, jnp.zeros((MODES, NB, LANES), F32), unroll=32)
            ends[s, u] = jnp.sum(acc * jnp.exp(spread(rate) * (sub - 7).astype(F32)), axis=1)
            return 0

        for u in range(CPS):
            group_pass(u, 0)

    def give_share(s):
        @pl.when(s != member)
        def _():
            pltpu.make_async_remote_copy(
                src_ref=ends.at[s], dst_ref=recv1.at[member], send_sem=s1.at[s], recv_sem=r1.at[member],
                device_id=member_dev(s), device_id_type=MESH,
            ).start()

        @pl.when(s == member)
        def _():
            recv1[member] = ends[s]

    def first_half(s, _):
        end_state(s)
        return 0

    def second_half(s, _):
        end_state(s)
        give_share(s)
        return 0

    lax.fori_loop(0, EARLY, first_half, 0)
    pl.semaphore_wait(barrier, 15)
    for s in range(EARLY):
        give_share(s)

    def load_w(half, n):
        start = (1 - t if half == 0 else t) * COLS + n * TILE
        cols = pl.ds(pl.multiple_of(start, TILE), TILE)
        return pltpu.make_async_copy(w_hbm.at[:, cols], wv.at[half, n], w_sem.at[half, n])

    for s in range(SHARES):
        load(2, q_hbm, qb, s).start()
    for half in range(2):
        for n in range(NT):
            load_w(half, n).start()

    lax.fori_loop(EARLY, SHARES, second_half, 0)

    def block_states(cg, _):
        cols = lanes(cg)
        rate = lam[:, cols]
        a = spread(jnp.exp(-rate))
        a_s[cg] = a
        for b in range(NB):
            rows = pl.ds(b * NJ, NJ)
            prod[cg, pl.ds(b, NJ, stride=NB), :] = kb[rows, cols].astype(F32) * vb[rows, cols].astype(F32)

        def step(j, acc):
            p = prod[cg, pl.ds(pl.multiple_of(j * NB, NB), NB), :]
            return acc * a + p[None]

        acc = lax.fori_loop(0, NJ, step, jnp.zeros((MODES, NB, LANES), F32), unroll=16)
        d1 = spread(jnp.exp(-float(NJ) * rate))
        d2 = d1 * d1
        acc = acc + jnp.where(sub >= 1, d1 * pltpu.roll(acc, 1, 1), 0.0)
        acc = acc + jnp.where(sub >= 2, d2 * pltpu.roll(acc, 2, 1), 0.0)
        acc = acc + jnp.where(sub >= 4, d2 * d2 * pltpu.roll(acc, 4, 1), 0.0)
        state[cg] = jnp.where(sub >= 1, pltpu.roll(acc, 1, 1), 0.0)
        return 0

    lax.fori_loop(0, SPLIT1, block_states, 0)

    def share_decay(span):
        return jnp.exp(-float(span) * lam[:, share_cols(member)])

    def halves(x):
        return jnp.stack([x[:, u * LANES:(u + 1) * LANES] for u in range(CPS)])

    d_dev = halves(share_decay(ROWS))
    d_grp = halves(share_decay(ROWS * 8))

    def wait_recv(buf, sem, i, ssem):
        pltpu.make_async_remote_copy(
            src_ref=buf.at[i], dst_ref=buf.at[i], send_sem=ssem.at[i], recv_sem=sem.at[i],
            device_id=partner, device_id_type=MESH,
        ).wait_recv()

    for i in range(1, 8):
        m = lax.rem(member + i, 8)
        wait_recv(recv1, r1, m, s1)
    total = recv1[0]
    for m in range(1, 8):
        total = total * d_dev + recv1[m]
    send2[...] = total
    recv2[group] = total

    def copy2(g):
        return pltpu.make_async_remote_copy(
            src_ref=send2, dst_ref=recv2.at[group], send_sem=s2.at[g], recv_sem=r2.at[group],
            device_id=group_dev(g), device_id_type=MESH,
        )

    for i in (4, 5, 3, 6, 2, 7, 1):
        copy2(lax.rem(group + i, 8)).start()

    lax.fori_loop(SPLIT1, SPLIT2, block_states, 0)

    for i in (1, 7, 2, 6, 3, 5, 4):
        wait_recv(recv2, r2, lax.rem(group + i, 8), s2)
    incoming = jnp.zeros((CPS, MODES, LANES), F32)
    for g in range(8):
        incoming = jnp.where(g < group, incoming * d_grp + recv2[g], incoming)
    for m in range(8):
        send3[m] = incoming
        if m < 7:
            incoming = incoming * d_dev + recv1[m]
    recv3[member] = send3[member]

    def copy3(m):
        return pltpu.make_async_remote_copy(
            src_ref=send3.at[m], dst_ref=recv3.at[member], send_sem=s3.at[m], recv_sem=r3.at[member],
            device_id=member_dev(m), device_id_type=MESH,
        )

    for i in (4, 5, 3, 6, 2, 7, 1):
        copy3(lax.rem(member + i, 8)).start()

    lax.fori_loop(SPLIT2, NCG, block_states, 0)

    def prepare(cg, _):
        cols = lanes(cg)
        rate = lam[:, cols]
        w_s[cg] = spread(res[:, cols] * jnp.sqrt(one_minus_exp_neg(2.0 * rate)))
        pw_s[cg] = jnp.exp(spread(rate) * (sub.astype(F32) * -float(NJ)))
        for b in range(NB):
            gate[cg, pl.ds(b, NJ, stride=NB), :] = qb[pl.ds(b * NJ, NJ), cols].astype(F32)
        return 0

    for s in range(SHARES):
        load(2, q_hbm, qb, s).wait()
    lax.fori_loop(0, NCG, prepare, 0)

    def second_pass(chunk, cg):
        cols = lanes(cg)
        a = a_s[cg]
        w = w_s[cg]
        gain = skip[:, cols]
        x = state[cg]
        for pair in range(JPC // 2):
            tiles = []
            for j in (2 * pair, 2 * pair + 1):
                rows = pl.ds(pl.multiple_of((chunk * JPC + j) * NB, NB), NB)
                p = prod[cg, rows, :]
                x = x * a + p[None]
                filtered = jnp.sum(x * w, axis=0) + gain * p
                tiles.append(gate[cg, rows, :] * filtered)
            rows = pl.ds(pl.multiple_of(chunk * CROWS + pair * 16, 16), 16)
            gated[rows, cols] = jnp.concatenate(tiles, axis=0).astype(BF16)
        state[cg] = x

    def chunk_rows(chunk):
        return pl.ds(pl.multiple_of(chunk * CROWS, CROWS), CROWS)

    def tile_lanes(n):
        return pl.ds(n * LPT, LPT)

    def piece(chunk, n):
        return pltpu.make_async_remote_copy(
            src_ref=send_p.at[tile_lanes(n), chunk_rows(chunk)], dst_ref=recv_p.at[tile_lanes(n), chunk_rows(chunk)],
            send_sem=sp.at[chunk, n], recv_sem=rp.at[chunk, n], device_id=partner, device_id_type=MESH,
        )

    def project(chunk, first=0):
        rows = chunk_rows(chunk)

        def other(n, _):
            sums = jnp.dot(gated[rows, :], wv[0, n], preferred_element_type=F32)
            for u in range(LPT):
                send_p[n * LPT + u, rows, :] = sums[:, u * LANES:(u + 1) * LANES]
            piece(chunk, n).start()
            return 0

        lax.fori_loop(first, NT, other, 0)

    def project_own(chunk):
        rows = chunk_rows(chunk)

        def own(n, _):
            sums = jnp.dot(gated[rows, :], wv[1, n], preferred_element_type=F32)
            for u in range(LPT):
                own_p[n * LPT + u, rows, :] = sums[:, u * LANES:(u + 1) * LANES]
            return 0

        lax.fori_loop(0, NT, own, 0)

    def begin(s, _):
        @pl.when(s != member)
        def _():
            wait_recv(recv3, r3, s, s3)

        def start(u, _):
            cg = s * CPS + u
            state[cg] = state[cg] + pw_s[cg] * spread(recv3[s, u])
            second_pass(0, cg)
            return 0

        return lax.fori_loop(0, CPS, start, 0)

    ready = (SHARES - 2) * CPS * LANES
    lax.fori_loop(0, SHARES - 2, begin, 0)
    load_w(0, 0).wait()
    early = jnp.dot(gated[:CROWS, :ready], wv[0, 0, :ready, :], preferred_element_type=F32)
    for u in range(LPT):
        send_p[u, :CROWS, :] = early[:, u * LANES:(u + 1) * LANES]
    lax.fori_loop(SHARES - 2, SHARES, begin, 0)
    late = jnp.dot(gated[:CROWS, ready:], wv[0, 0, ready:, :], preferred_element_type=F32)
    for u in range(LPT):
        send_p[u, :CROWS, :] += late[:, u * LANES:(u + 1) * LANES]
    piece(0, 0).start()
    for n in range(1, NT):
        load_w(0, n).wait()
    project(0, 1)
    for n in range(NT):
        load_w(1, n).wait()
    project_own(0)

    def chunk_step(chunk, _):
        def one(cg, _):
            second_pass(chunk, cg)
            return 0

        lax.fori_loop(0, NCG, one, 0)
        project(chunk)
        project_own(chunk)
        return 0

    lax.fori_loop(1, NCHUNK, chunk_step, 0)

    def finish(i, _):
        h, n = i // NT, lax.rem(i, NT)
        piece(2 * h, n).wait_recv()
        piece(2 * h + 1, n).wait_recv()

        for u in range(LPT):
            k = n * LPT + u
            for b in range(NB):
                rows = pl.ds(h * (2 * CROWS) + b, 16, stride=NB)
                out_v[b, pl.ds(pl.multiple_of(h * 16, 16), 16), lanes(k)] = (own_p[k, rows, :] + recv_p[k, rows, :]).astype(BF16)
        return 0

    lax.fori_loop(0, (NCHUNK // 2) * NT, finish, 0)

    for i in range(1, 8):
        m = lax.rem(member + i, 8)
        g = lax.rem(group + i, 8)
        pltpu.make_async_remote_copy(
            src_ref=ends.at[m], dst_ref=recv1.at[member], send_sem=s1.at[m], recv_sem=r1.at[member],
            device_id=member_dev(m), device_id_type=MESH,
        ).wait_send()
        copy2(g).wait_send()
        copy3(m).wait_send()

    def drain(i, _):
        piece(i // NT, lax.rem(i, NT)).wait_send()
        return 0

    lax.fori_loop(0, NCHUNK * NT, drain, 0)


def per_device(query_gate, key_gate, value_input, decay_rates, residues, skip_gain, out_weight):
    dma = pltpu.SemaphoreType.DMA
    out = pl.pallas_call(
        kernel,
        out_shape=pltpu.VMEM((NB, NJ, COLS), BF16),
        in_specs=[pl.BlockSpec(memory_space=pl.ANY)] * 7,
        out_specs=pl.BlockSpec(memory_space=pltpu.VMEM),
        scratch_shapes=[
            pltpu.VMEM((ROWS, CHAN), BF16),
            pltpu.VMEM((ROWS, CHAN), BF16),
            pltpu.VMEM((ROWS, CHAN), BF16),
            pltpu.VMEM((MODES, CHAN), F32),
            pltpu.VMEM((MODES, CHAN), F32),
            pltpu.VMEM((1, CHAN), F32),
            pltpu.VMEM((2, NT, CHAN, TILE), BF16),
            pltpu.VMEM((NCG, ROWS, LANES), F32),
            pltpu.VMEM((NCG, ROWS, LANES), F32),
            pltpu.VMEM((ROWS, CHAN), BF16),
            pltpu.VMEM((COLS // LANES, ROWS, LANES), F32),
            pltpu.VMEM((COLS // LANES, ROWS, LANES), F32),
            pltpu.VMEM((COLS // LANES, ROWS, LANES), F32),
            pltpu.VMEM((NCG, MODES, NB, LANES), F32),
            pltpu.VMEM((NCG, MODES, NB, LANES), F32),
            pltpu.VMEM((NCG, MODES, NB, LANES), F32),
            pltpu.VMEM((NCG, MODES, NB, LANES), F32),
            pltpu.VMEM((SHARES, CPS, MODES, LANES), F32),
            pltpu.VMEM((8, CPS, MODES, LANES), F32),
            pltpu.VMEM((8, CPS, MODES, LANES), F32),
            pltpu.VMEM((8, CPS, MODES, LANES), F32),
            pltpu.VMEM((CPS, MODES, LANES), F32),
            pltpu.VMEM((8, CPS, MODES, LANES), F32),
            dma((4, SHARES)), dma((2, NT)),
            dma((8,)), dma((8,)), dma((8,)), dma((8,)), dma((8,)), dma((8,)),
            dma((NCHUNK, NT)), dma((NCHUNK, NT)),
        ],
        compiler_params=pltpu.CompilerParams(
            collective_id=0, has_side_effects=True, vmem_limit_bytes=56 * 2**20
        ),
    )(
        query_gate, key_gate, value_input, decay_rates, residues, skip_gain.reshape(1, CHAN), out_weight
    )
    return out.reshape(ROWS, COLS)


def solution(mesh):
    in_specs = (
        P("ctx", "tp"),
        P("ctx", "tp"),
        P("ctx", "tp"),
        P(None, "tp"),
        P(None, "tp"),
        P("tp"),
        P("tp", None),
    )
    return jax.shard_map(per_device, mesh=mesh, in_specs=in_specs, out_specs=P("ctx", "tp"), check_vma=False)
```

```python
import jax
import jax.numpy as jnp
from jax import lax
from jax.experimental import pallas as pl
from jax.experimental.pallas import tpu as pltpu
from jax.sharding import PartitionSpec as P

MESH = pl.DeviceIdType.MESH
F32 = jnp.float32
BF16 = jnp.bfloat16

ROWS = 512
CHAN = 2048
COLS = 2048
MODES = 16
LANES = 128
NB = 8
NJ = ROWS // NB
NCG = CHAN // LANES
SHARES = 8
CPS = NCG // SHARES
JPC = 8
NCHUNK = NJ // JPC
CROWS = JPC * NB
TILE = 512
NT = COLS // TILE
LPT = TILE // LANES
EARLY = 4
SPLIT1, SPLIT2 = 4, 13


def one_minus_exp_neg(y):
    series = jnp.ones_like(y)
    for k in range(10, 1, -1):
        series = 1.0 - y * series * (1.0 / k)
    return jnp.where(y < 0.5, y * series, 1.0 - jnp.exp(-y))


def spread(x):
    return jnp.broadcast_to(x[:, None, :], (MODES, NB, LANES))


def kernel(
    q_hbm, k_hbm, v_hbm, lam_hbm, res_hbm, skip_hbm, w_hbm, out_v,
    qb, kb, vb, lam, res, skip, wv, prod, gate, gated, send_p, recv_p, own_p,
    a_s, w_s, pw_s, state, ends, recv1, recv2, recv3, send2, send3,
    in_sem, w_sem, s1, r1, s2, r2, s3, r3, sp, rp,
):
    c = lax.axis_index("ctx")
    t = lax.axis_index("tp")
    member = lax.rem(c, 8)
    yh = lax.rem(c // 8, 2)
    z = c // 16
    group = z * 2 + yh
    base = c - member

    def member_dev(m):
        return (base + m, t)

    def group_dev(g):
        return (g * 8 + member, t)

    partner = (c, 1 - t)

    def lanes(cg):
        return pl.ds(pl.multiple_of(cg * LANES, LANES), LANES)

    def share_cols(s):
        return pl.ds(pl.multiple_of(s * (CPS * LANES), CPS * LANES), CPS * LANES)

    small = [
        pltpu.make_async_copy(lam_hbm, lam, in_sem.at[3, 0]),
        pltpu.make_async_copy(res_hbm, res, in_sem.at[3, 1]),
        pltpu.make_async_copy(skip_hbm, skip, in_sem.at[3, 2]),
    ]
    for cp in small:
        cp.start()

    def load(which, hbm, dst, s):
        return pltpu.make_async_copy(hbm.at[:, share_cols(s)], dst.at[:, share_cols(s)], in_sem.at[which, s])

    for s in range(SHARES):
        load(0, k_hbm, kb, s).start()
        load(1, v_hbm, vb, s).start()

    barrier = pltpu.get_barrier_semaphore()
    for i in range(1, 8):
        pl.semaphore_signal(barrier, inc=1, device_id=member_dev(lax.rem(member + i, 8)), device_id_type=MESH)
        pl.semaphore_signal(barrier, inc=1, device_id=group_dev(lax.rem(group + i, 8)), device_id_type=MESH)
    pl.semaphore_signal(barrier, inc=1, device_id=partner, device_id_type=MESH)

    for cp in small:
        cp.wait()

    sub = lax.broadcasted_iota(jnp.int32, (MODES, NB, LANES), 1)

    def end_state(s):
        load(0, k_hbm, kb, s).wait()
        load(1, v_hbm, vb, s).wait()

        def group_pass(u, _):
            cols = lanes(s * CPS + u)
            rate = lam[:, cols]
            a8 = spread(jnp.exp(-8.0 * rate))
            a16 = a8 * a8

            def step(i, acc):
                rows = pl.ds(pl.multiple_of(i * 16, 16), 16)
                p = kb[rows, cols].astype(F32) * vb[rows, cols].astype(F32)
                return acc * a16 + (p[None, :8] * a8 + p[None, 8:])

            acc = lax.fori_loop(0, ROWS // 16, step, jnp.zeros((MODES, NB, LANES), F32), unroll=32)
            ends[s, u] = jnp.sum(acc * jnp.exp(spread(rate) * (sub - 7).astype(F32)), axis=1)
            return 0

        for u in range(CPS):
            group_pass(u, 0)

    def give_share(s):
        @pl.when(s != member)
        def _():
            pltpu.make_async_remote_copy(
                src_ref=ends.at[s], dst_ref=recv1.at[member], send_sem=s1.at[s], recv_sem=r1.at[member],
                device_id=member_dev(s), device_id_type=MESH,
            ).start()

        @pl.when(s == member)
        def _():
            recv1[member] = ends[s]

    def first_half(s, _):
        end_state(s)
        return 0

    def second_half(s, _):
        end_state(s)
        give_share(s)
        return 0

    lax.fori_loop(0, EARLY, first_half, 0)
    pl.semaphore_wait(barrier, 15)
    for s in range(EARLY):
        give_share(s)

    def load_w(half, n):
        start = (1 - t if half == 0 else t) * COLS + n * TILE
        cols = pl.ds(pl.multiple_of(start, TILE), TILE)
        return pltpu.make_async_copy(w_hbm.at[:, cols], wv.at[half, n], w_sem.at[half, n])

    for s in range(SHARES):
        load(2, q_hbm, qb, s).start()
    for half in range(2):
        for n in range(NT):
            load_w(half, n).start()

    lax.fori_loop(EARLY, SHARES, second_half, 0)

    def block_states(cg, _):
        cols = lanes(cg)
        rate = lam[:, cols]
        a = spread(jnp.exp(-rate))
        a_s[cg] = a
        for b in range(NB):
            rows = pl.ds(b * NJ, NJ)
            prod[cg, pl.ds(b, NJ, stride=NB), :] = kb[rows, cols].astype(F32) * vb[rows, cols].astype(F32)

        def step(j, acc):
            p = prod[cg, pl.ds(pl.multiple_of(j * NB, NB), NB), :]
            return acc * a + p[None]

        acc = lax.fori_loop(0, NJ, step, jnp.zeros((MODES, NB, LANES), F32), unroll=16)
        d1 = spread(jnp.exp(-float(NJ) * rate))
        d2 = d1 * d1
        acc = acc + jnp.where(sub >= 1, d1 * pltpu.roll(acc, 1, 1), 0.0)
        acc = acc + jnp.where(sub >= 2, d2 * pltpu.roll(acc, 2, 1), 0.0)
        acc = acc + jnp.where(sub >= 4, d2 * d2 * pltpu.roll(acc, 4, 1), 0.0)
        state[cg] = jnp.where(sub >= 1, pltpu.roll(acc, 1, 1), 0.0)
        return 0

    lax.fori_loop(0, SPLIT1, block_states, 0)

    def share_decay(span):
        return jnp.exp(-float(span) * lam[:, share_cols(member)])

    def halves(x):
        return jnp.stack([x[:, u * LANES:(u + 1) * LANES] for u in range(CPS)])

    d_dev = halves(share_decay(ROWS))
    d_grp = halves(share_decay(ROWS * 8))

    def wait_recv(buf, sem, i, ssem):
        pltpu.make_async_remote_copy(
            src_ref=buf.at[i], dst_ref=buf.at[i], send_sem=ssem.at[i], recv_sem=sem.at[i],
            device_id=partner, device_id_type=MESH,
        ).wait_recv()

    for i in range(1, 8):
        m = lax.rem(member + i, 8)
        wait_recv(recv1, r1, m, s1)
    total = recv1[0]
    for m in range(1, 8):
        total = total * d_dev + recv1[m]
    send2[...] = total
    recv2[group] = total

    def copy2(g):
        return pltpu.make_async_remote_copy(
            src_ref=send2, dst_ref=recv2.at[group], send_sem=s2.at[g], recv_sem=r2.at[group],
            device_id=group_dev(g), device_id_type=MESH,
        )

    for i in (4, 5, 3, 6, 2, 7, 1):
        copy2(lax.rem(group + i, 8)).start()

    lax.fori_loop(SPLIT1, SPLIT2, block_states, 0)

    for i in (1, 7, 2, 6, 3, 5, 4):
        wait_recv(recv2, r2, lax.rem(group + i, 8), s2)
    incoming = jnp.zeros((CPS, MODES, LANES), F32)
    for g in range(8):
        incoming = jnp.where(g < group, incoming * d_grp + recv2[g], incoming)
    for m in range(8):
        send3[m] = incoming
        if m < 7:
            incoming = incoming * d_dev + recv1[m]
    recv3[member] = send3[member]

    def copy3(m):
        return pltpu.make_async_remote_copy(
            src_ref=send3.at[m], dst_ref=recv3.at[member], send_sem=s3.at[m], recv_sem=r3.at[member],
            device_id=member_dev(m), device_id_type=MESH,
        )

    for i in (4, 5, 3, 6, 2, 7, 1):
        copy3(lax.rem(member + i, 8)).start()

    lax.fori_loop(SPLIT2, NCG, block_states, 0)

    def prepare(cg, _):
        cols = lanes(cg)
        rate = lam[:, cols]
        w_s[cg] = spread(res[:, cols] * jnp.sqrt(one_minus_exp_neg(2.0 * rate)))
        pw_s[cg] = jnp.exp(spread(rate) * (sub.astype(F32) * -float(NJ)))
        for b in range(NB):
            gate[cg, pl.ds(b, NJ, stride=NB), :] = qb[pl.ds(b * NJ, NJ), cols].astype(F32)
        return 0

    for s in range(SHARES):
        load(2, q_hbm, qb, s).wait()
    lax.fori_loop(0, NCG, prepare, 0)

    def second_pass(chunk, cg):
        cols = lanes(cg)
        a = a_s[cg]
        w = w_s[cg]
        gain = skip[:, cols]
        x = state[cg]
        for pair in range(JPC // 2):
            tiles = []
            for j in (2 * pair, 2 * pair + 1):
                rows = pl.ds(pl.multiple_of((chunk * JPC + j) * NB, NB), NB)
                p = prod[cg, rows, :]
                x = x * a + p[None]
                filtered = jnp.sum(x * w, axis=0) + gain * p
                tiles.append(gate[cg, rows, :] * filtered)
            rows = pl.ds(pl.multiple_of(chunk * CROWS + pair * 16, 16), 16)
            gated[rows, cols] = jnp.concatenate(tiles, axis=0).astype(BF16)
        state[cg] = x

    def chunk_rows(chunk):
        return pl.ds(pl.multiple_of(chunk * CROWS, CROWS), CROWS)

    def tile_lanes(n):
        return pl.ds(n * LPT, LPT)

    def piece(chunk, n):
        return pltpu.make_async_remote_copy(
            src_ref=send_p.at[tile_lanes(n), chunk_rows(chunk)], dst_ref=recv_p.at[tile_lanes(n), chunk_rows(chunk)],
            send_sem=sp.at[chunk, n], recv_sem=rp.at[chunk, n], device_id=partner, device_id_type=MESH,
        )

    def project(chunk, first=0):
        rows = chunk_rows(chunk)

        def other(n, _):
            sums = jnp.dot(gated[rows, :], wv[0, n], preferred_element_type=F32)
            for u in range(LPT):
                send_p[n * LPT + u, rows, :] = sums[:, u * LANES:(u + 1) * LANES]
            piece(chunk, n).start()
            return 0

        lax.fori_loop(first, NT, other, 0)

    def project_own(chunk):
        rows = chunk_rows(chunk)

        def own(n, _):
            sums = jnp.dot(gated[rows, :], wv[1, n], preferred_element_type=F32)
            for u in range(LPT):
                own_p[n * LPT + u, rows, :] = sums[:, u * LANES:(u + 1) * LANES]
            return 0

        lax.fori_loop(0, NT, own, 0)

    def begin(s, _):
        @pl.when(s != member)
        def _():
            wait_recv(recv3, r3, s, s3)

        def start(u, _):
            cg = s * CPS + u
            state[cg] = state[cg] + pw_s[cg] * spread(recv3[s, u])
            second_pass(0, cg)
            return 0

        return lax.fori_loop(0, CPS, start, 0)

    ready = (SHARES - 2) * CPS * LANES
    lax.fori_loop(0, SHARES - 2, begin, 0)
    load_w(0, 0).wait()
    early = jnp.dot(gated[:CROWS, :ready], wv[0, 0, :ready, :], preferred_element_type=F32)
    for u in range(LPT):
        send_p[u, :CROWS, :] = early[:, u * LANES:(u + 1) * LANES]
    lax.fori_loop(SHARES - 2, SHARES, begin, 0)
    late = jnp.dot(gated[:CROWS, ready:], wv[0, 0, ready:, :], preferred_element_type=F32)
    for u in range(LPT):
        send_p[u, :CROWS, :] += late[:, u * LANES:(u + 1) * LANES]
    piece(0, 0).start()
    for n in range(1, NT):
        load_w(0, n).wait()
    project(0, 1)
    for n in range(NT):
        load_w(1, n).wait()
    project_own(0)

    def chunk_step(chunk, _):
        def one(cg, _):
            second_pass(chunk, cg)
            return 0

        lax.fori_loop(0, NCG, one, 0)
        project(chunk)
        project_own(chunk)
        return 0

    lax.fori_loop(1, NCHUNK, chunk_step, 0)

    for i in range(1, 8):
        m = lax.rem(member + i, 8)
        g = lax.rem(group + i, 8)
        pltpu.make_async_remote_copy(
            src_ref=ends.at[m], dst_ref=recv1.at[member], send_sem=s1.at[m], recv_sem=r1.at[member],
            device_id=member_dev(m), device_id_type=MESH,
        ).wait_send()
        copy2(g).wait_send()
        copy3(m).wait_send()

    def finish(i, _):
        h, n = i // NT, lax.rem(i, NT)
        piece(2 * h, n).wait()
        piece(2 * h + 1, n).wait()

        for u in range(LPT):
            k = n * LPT + u
            for b in range(NB):
                rows = pl.ds(h * (2 * CROWS) + b, 16, stride=NB)
                out_v[b, pl.ds(pl.multiple_of(h * 16, 16), 16), lanes(k)] = (own_p[k, rows, :] + recv_p[k, rows, :]).astype(BF16)
        return 0

    lax.fori_loop(0, (NCHUNK // 2) * NT, finish, 0)


def per_device(query_gate, key_gate, value_input, decay_rates, residues, skip_gain, out_weight):
    dma = pltpu.SemaphoreType.DMA
    out = pl.pallas_call(
        kernel,
        out_shape=pltpu.VMEM((NB, NJ, COLS), BF16),
        in_specs=[pl.BlockSpec(memory_space=pl.ANY)] * 7,
        out_specs=pl.BlockSpec(memory_space=pltpu.VMEM),
        scratch_shapes=[
            pltpu.VMEM((ROWS, CHAN), BF16),
            pltpu.VMEM((ROWS, CHAN), BF16),
            pltpu.VMEM((ROWS, CHAN), BF16),
            pltpu.VMEM((MODES, CHAN), F32),
            pltpu.VMEM((MODES, CHAN), F32),
            pltpu.VMEM((1, CHAN), F32),
            pltpu.VMEM((2, NT, CHAN, TILE), BF16),
            pltpu.VMEM((NCG, ROWS, LANES), F32),
            pltpu.VMEM((NCG, ROWS, LANES), F32),
            pltpu.VMEM((ROWS, CHAN), BF16),
            pltpu.VMEM((COLS // LANES, ROWS, LANES), F32),
            pltpu.VMEM((COLS // LANES, ROWS, LANES), F32),
            pltpu.VMEM((COLS // LANES, ROWS, LANES), F32),
            pltpu.VMEM((NCG, MODES, NB, LANES), F32),
            pltpu.VMEM((NCG, MODES, NB, LANES), F32),
            pltpu.VMEM((NCG, MODES, NB, LANES), F32),
            pltpu.VMEM((NCG, MODES, NB, LANES), F32),
            pltpu.VMEM((SHARES, CPS, MODES, LANES), F32),
            pltpu.VMEM((8, CPS, MODES, LANES), F32),
            pltpu.VMEM((8, CPS, MODES, LANES), F32),
            pltpu.VMEM((8, CPS, MODES, LANES), F32),
            pltpu.VMEM((CPS, MODES, LANES), F32),
            pltpu.VMEM((8, CPS, MODES, LANES), F32),
            dma((4, SHARES)), dma((2, NT)),
            dma((8,)), dma((8,)), dma((8,)), dma((8,)), dma((8,)), dma((8,)),
            dma((NCHUNK, NT)), dma((NCHUNK, NT)),
        ],
        compiler_params=pltpu.CompilerParams(
            collective_id=0, has_side_effects=True, vmem_limit_bytes=56 * 2**20
        ),
    )(
        query_gate, key_gate, value_input, decay_rates, residues, skip_gain.reshape(1, CHAN), out_weight
    )
    return out.reshape(ROWS, COLS)


def solution(mesh):
    in_specs = (
        P("ctx", "tp"),
        P("ctx", "tp"),
        P("ctx", "tp"),
        P(None, "tp"),
        P(None, "tp"),
        P("tp"),
        P("tp", None),
    )
    return jax.shard_map(per_device, mesh=mesh, in_specs=in_specs, out_specs=P("ctx", "tp"), check_vma=False)
```
